32 devices in a mesh: grp: 2 (over y), user: 4 (over z), tm: 4 (over x, core).
Axes of the slice: x: 2, y: 2, z: 4, core: 2. Of those that a mesh axis runs over, the one named last changes fastest.
Arguments:
- history: bfloat16 [8, 1024, 512], P(('grp', 'user'), 'tm'), parts along dimension 0, may hold values from -6 to 6
- z_weight: bfloat16 [512, 1024], replicated, may hold values from -0.25 to 0.25
- xbc_weight: bfloat16 [512, 1280], replicated, may hold values from -0.25 to 0.25
- dt_weight: bfloat16 [512, 16], replicated, may hold values from -0.125 to 0.125
- dt_bias: float32 [16], replicated, may hold values from -1 to 0.5
- a_log: float32 [16], replicated
- conv_weight: float32 [4, 1280], replicated, may hold values from -3 to 3
- conv_bias: float32 [1280], replicated, may hold values from -3 to 3
- d_skip: float32 [16], replicated, may hold values from 0.5 to 1.5
- norm_gain: float32 [1024], replicated, may hold values from 0.1 to 1.9
- out_weight: bfloat16 [1024, 512], replicated, may hold values from -0.1875 to 0.1875
- label_pos: int32 [8, 2048], P(('grp', 'user'), 'tm'), parts along dimension 0, may hold values from 0 to 1023, as said below
- label_count: int32 [8, 4], P(('grp', 'user'), 'tm'), parts along dimension 0, may hold values from 1 to 511, as said below
- label_value: int32 [8, 2048], P(('grp', 'user'), 'tm'), parts along dimension 0, may hold values 0 or 1
- item_feat: bfloat16 [8, 2048, 512], P(('grp', 'user'), 'tm'), parts along dimension 0, may hold values from -6 to 6
- first_weight: bfloat16 [1024, 1024], replicated, may hold values from -0.1875 to 0.1875
- second_weight: bfloat16 [1024], replicated, may hold values from -0.1875 to 0.1875
Outputs:
- encoded: bfloat16 [8, 1024, 512], P(('grp', 'user'), 'tm'), parts along dimension 0
- row_logit: float32 [8, 2048], P(('grp', 'user'), 'tm'), parts along dimension 0
- grad_first: float32 [2048, 1024], P('grp'), parts along dimension 0
- grad_second: float32 [2048], P('grp'), parts along dimension 0
The draws below stay inside these ranges and needn't reach their ends.
There are 2 independent parts, one for each index of `grp`. The reference program is written for one: setup_inputs(seed, part) draws one part's arguments, and reference() takes and returns one part's arrays. A program takes and returns all parts, laid end to end along the dimension named above; an argument that names none is the same for every part. Nothing has to cross between parts.
Inputs may be any that keep to these rules, and one draw needn't show every extreme that they name: `label_pos`: positions in slots k * 512 to (k + 1) * 512 - 1 of a user lie in events k * 256 to (k + 1) * 256 - 1. label_count[u, k] slots are used in block k of user u's slots, and they are the block's first ones; the counts of blocks 2 * k and 2 * k + 1 of a user sum to 512.
All inputs are finite; a program needn't handle non-finite values. No bound on the sum of `label_value` on one device may be relied on, other than what follows from the above.
Results may differ from the reference program's by a relative error of at most 0.015.
Values may be sent and summed in bfloat16 or wider, within the bound.
A program may use at most 64 MiB of HBM per device.

```python
import jax
import jax.numpy as jnp
from jax import lax

D = 512
HEADS = 16
HDIM = 64
DSTATE = 128
CONV = 4
BLOCK = 256
HID = 1024
L_DEV = 256
DINNER = 1024
XBC = 1280
LENGTH = 1024
USERS = 4
LAB_DEV = 512
SLOTS = 2048
N_TM = 4


def draw_a_log(key, part):
    pick_key, fast_key, slow_key = jax.random.split(key, 3)
    portion = 0.5
    slow_heads = jax.random.uniform(pick_key, (HEADS,)) < portion
    fast_rate = jax.random.uniform(fast_key, (HEADS,), minval=0.04, maxval=0.08)
    slow_rate = jax.random.uniform(slow_key, (HEADS,), minval=0.2, maxval=1.0) / LENGTH
    return jnp.log(jnp.where(slow_heads, slow_rate, fast_rate)).astype(jnp.float32)


def draw_label_pos(key, part):
    offsets = jax.random.randint(key, (USERS, SLOTS), 0, L_DEV)
    starts = jnp.arange(SLOTS, dtype=jnp.int32) // LAB_DEV * L_DEV
    places = offsets + starts[None, :]
    places = places.at[:, 0].set(0)
    places = places.at[:, SLOTS - 1].set(LENGTH - 1)
    return places.astype(jnp.int32)


def draw_label_count(key, part):
    pair_count = N_TM // 2
    first_key, forced_key, side_key = jax.random.split(jax.random.fold_in(key, 17), 3)
    first = jax.random.randint(first_key, (USERS, pair_count), 1, LAB_DEV)
    forced = jax.random.randint(forced_key, (USERS,), 0, pair_count)
    side = jax.random.randint(side_key, (USERS,), 0, 2)
    extreme = jnp.where(side == 1, LAB_DEV - 1, 1)
    pair_iota = jnp.arange(pair_count, dtype=jnp.int32)
    first = jnp.where(pair_iota[None, :] == forced[:, None], extreme[:, None], first)
    paired = jnp.stack([first, LAB_DEV - first], axis=2)
    return paired.reshape(USERS, N_TM).astype(jnp.int32)


def plant(drawn, stream_key, low, top_value):
    extent = drawn.shape
    index_at = [jax.random.randint(jax.random.fold_in(stream_key, axis), (), 0, extent[axis]) for axis in range(len(extent))]
    drawn = drawn.at[tuple(index_at)].set(low)
    longest = extent.index(max(extent))
    index_at[longest] = (index_at[longest] + 1) % extent[longest]
    return drawn.at[tuple(index_at)].set(top_value)


def shard_levels(own_key, extent, shards, low, top_value):
    def one(dim, parts):
        steps = jax.random.uniform(jax.random.fold_in(jax.random.fold_in(own_key, 6), dim), (parts,), jnp.float32, low / len(shards), top_value / len(shards))
        return jnp.repeat(jnp.exp(steps), extent[dim] // parts).reshape((-1,) + (1,) * (len(extent) - dim - 1))

    factor_of = one(*shards[0])
    for cut in shards[1:]:
        factor_of = factor_of * one(*cut)
    return factor_of


def gaussian(stream_key, dims, spread, most, cuts=(), held_as=jnp.bfloat16):
    loudness = shard_levels(stream_key, dims, cuts, -0.22, 0.18) if cuts else 1.0
    values = jax.random.normal(stream_key, dims, jnp.float32) * spread * loudness
    return jnp.minimum(jnp.maximum(values, -most), most).astype(held_as)


def setup_inputs(seed: int = 0, part: int = 0) -> dict:
    seeds = jax.random.split(jax.random.key(seed), 18)
    own_keys = jax.random.split(jax.random.fold_in(seeds[17], part), 18)
    return {
        "history": gaussian(own_keys[0], (USERS, LENGTH, D), 1.0, 6.0, ((0, 4), (1, 4))),
        "z_weight": gaussian(seeds[1], (D, DINNER), D ** -0.5, 0.25),
        "xbc_weight": gaussian(seeds[2], (D, XBC), D ** -0.5, 0.25),
        "dt_weight": gaussian(seeds[3], (D, HEADS), (4 * D) ** -0.5, 0.125),
        "dt_bias": jnp.clip(jax.random.uniform(seeds[4], (HEADS,), jnp.float32, -1.0, 0.5), -1.0, 0.5),
        "a_log": draw_a_log(jax.random.fold_in(seeds[17], 71), part),
        "conv_weight": gaussian(seeds[6], (CONV, XBC), 0.5, 3.0, (), jnp.float32),
        "conv_bias": gaussian(seeds[7], (XBC,), 0.5, 3.0, (), jnp.float32),
        "d_skip": jnp.clip(jax.random.uniform(seeds[8], (HEADS,), jnp.float32, 0.5, 1.5), 0.5, 1.5),
        "norm_gain": jnp.clip(1.0 + 0.18 * jax.random.normal(seeds[9], (DINNER,), jnp.float32), 0.1, 1.9),
        "out_weight": gaussian(seeds[10], (DINNER, D), DINNER ** -0.5, 0.1875),
        "label_pos": draw_label_pos(jax.random.fold_in(jax.random.fold_in(seeds[17], part), 71), part),
        "label_count": draw_label_count(jax.random.fold_in(jax.random.fold_in(seeds[17], part), 71), part),
        "label_value": plant((jax.random.randint(own_keys[13], (USERS, SLOTS), 0, 2) < 1).astype(jnp.int32), jax.random.fold_in(own_keys[13], 1), 0, 1),
        "item_feat": gaussian(own_keys[14], (USERS, SLOTS, D), 1.0, 6.0, ((0, 4), (1, 4))),
        "first_weight": gaussian(seeds[15], (2 * D, HID), (2 * D) ** -0.5, 0.1875),
        "second_weight": gaussian(seeds[16], (HID,), HID ** -0.5, 0.1875),
    }


def silu_grad(values):
    sig = jax.nn.sigmoid(values)
    return sig * (1.0 + values * (1.0 - sig))

def ranker(rank_rows, target, live_mask, first_weight, second_weight):
    pre_act = jnp.dot(rank_rows, first_weight, preferred_element_type=jnp.float32)
    hidden = jax.nn.silu(pre_act).astype(jnp.bfloat16)
    logit_vec = jnp.dot(hidden, second_weight, preferred_element_type=jnp.float32)
    dlogit = live_mask * (jax.nn.sigmoid(logit_vec) - target)
    grad_two = jnp.dot(dlogit, hidden.astype(jnp.float32), precision=lax.Precision.HIGHEST)
    grad_pre = (dlogit[:, None] * second_weight.astype(jnp.float32)[None, :] * silu_grad(pre_act)).astype(jnp.bfloat16)
    grad_one = jnp.dot(rank_rows.T, grad_pre, preferred_element_type=jnp.float32)
    return (live_mask * logit_vec, grad_one, grad_two)

def encode_user(history_user, z_weight, xbc_weight, dt_weight, dt_bias, a_log, conv_weight, conv_bias, d_skip, norm_gain, out_weight):
    z_gate = jnp.dot(history_user, z_weight, preferred_element_type=jnp.float32).astype(jnp.bfloat16)
    xbc_raw = jnp.dot(history_user, xbc_weight, preferred_element_type=jnp.float32).astype(jnp.bfloat16)
    step_size = jax.nn.softplus(jnp.dot(history_user, dt_weight, preferred_element_type=jnp.float32) + dt_bias)
    padded = jnp.concatenate([jnp.zeros((CONV - 1, XBC), jnp.bfloat16), xbc_raw], axis=0)
    conv_sum = jnp.zeros((LENGTH, XBC), jnp.float32) + conv_bias[None, :]
    for tap in range(CONV):
        conv_sum = conv_sum + conv_weight[tap][None, :] * padded[tap:tap + LENGTH].astype(jnp.float32)
    xbc = jax.nn.silu(conv_sum).astype(jnp.bfloat16)
    block_count = LENGTH // BLOCK
    x_part = xbc[:, :DINNER].reshape(block_count, BLOCK, HEADS, HDIM)
    b_part = xbc[:, DINNER:DINNER + DSTATE].reshape(block_count, BLOCK, DSTATE)
    c_part = xbc[:, DINNER + DSTATE:].reshape(block_count, BLOCK, DSTATE)
    log_decay = (-jnp.exp(a_log)[None, :] * step_size).reshape(block_count, BLOCK, HEADS)
    cumulated = jnp.cumsum(log_decay, axis=1)
    step_blocks = step_size.reshape(block_count, BLOCK, HEADS)
    rows_idx = lax.broadcasted_iota(jnp.int32, (BLOCK, BLOCK), 0)
    cols_idx = lax.broadcasted_iota(jnp.int32, (BLOCK, BLOCK), 1)
    causal = (cols_idx <= rows_idx)[None]

    def block_step(carry_state, inputs):
        x_block, b_block, c_block, cum_block, step_block = inputs
        scores = jnp.dot(c_block, b_block.T, preferred_element_type=jnp.float32)
        cum_heads = cum_block.T
        gaps = cum_heads[:, :, None] - cum_heads[:, None, :]
        decays = jnp.where(causal, jnp.exp(jnp.where(causal, gaps, 0.0)), 0.0)
        weights = (decays * step_block.T[:, None, :] * scores[None]).astype(jnp.bfloat16)
        within = jnp.einsum('hts,shp->thp', weights.astype(jnp.float32), x_block.astype(jnp.float32))
        last_cum = cum_block[-1]
        across = jnp.exp(cum_block)[:, :, None] * jnp.einsum('tn,hpn->thp', c_block.astype(jnp.float32), carry_state, precision=lax.Precision.HIGHEST)
        carried = ((jnp.exp(last_cum[None, :] - cum_block) * step_block)[:, :, None] * x_block.astype(jnp.float32)).astype(jnp.bfloat16)
        new_state = jnp.exp(last_cum)[:, None, None] * carry_state + jnp.einsum('shp,sn->hpn', carried.astype(jnp.float32), b_block.astype(jnp.float32))
        result = within + across + d_skip[None, :, None] * x_block.astype(jnp.float32)
        return (new_state, result)
    zero_state = jnp.zeros((HEADS, HDIM, DSTATE), jnp.float32)
    final_state, ssd_out = lax.scan(block_step, zero_state, (x_part, b_part, c_part, cumulated, step_blocks))
    ssd_out = ssd_out.reshape(LENGTH, DINNER)
    gated_out = ssd_out * jax.nn.silu(z_gate.astype(jnp.float32))
    normed = (gated_out * lax.rsqrt(lax.optimization_barrier(jnp.mean(gated_out * gated_out, axis=-1, keepdims=True)) + 1e-05) * norm_gain[None, :]).astype(jnp.bfloat16)
    return jnp.dot(normed, out_weight, preferred_element_type=jnp.float32).astype(jnp.bfloat16)

def reference(history, z_weight, xbc_weight, dt_weight, dt_bias, a_log, conv_weight, conv_bias, d_skip, norm_gain, out_weight, label_pos, label_count, label_value, item_feat, first_weight, second_weight):
    slot_ids = jnp.arange(SLOTS).astype(jnp.int32)

    def per_user(carry, inputs):
        history_user, pos_user, count_user, value_user, item_user = inputs
        encoded_user = encode_user(history_user, z_weight, xbc_weight, dt_weight, dt_bias, a_log, conv_weight, conv_bias, d_skip, norm_gain, out_weight)
        enc_rows = encoded_user[pos_user]
        rank_rows = jnp.concatenate([enc_rows, item_user], axis=-1)
        live_mask = (slot_ids % LAB_DEV < count_user[slot_ids // LAB_DEV]).astype(jnp.float32)
        logit_vec, grad_one, grad_two = ranker(rank_rows, value_user.astype(jnp.float32), live_mask, first_weight, second_weight)
        return ((carry[0] + grad_one, carry[1] + grad_two), (encoded_user, logit_vec))
    start = (jnp.zeros((2 * D, HID), jnp.float32), jnp.zeros((HID,), jnp.float32))
    grads, outputs = lax.scan(per_user, start, (history, label_pos, label_count, label_value, item_feat))
    return (outputs[0], outputs[1], grads[0], grads[1])
```

```python
import functools

import jax
import jax.numpy as jnp
from jax import lax
from jax.experimental import pallas as pl
from jax.experimental.pallas import tpu as pltpu
from jax.sharding import PartitionSpec as P

F32, BF16 = jnp.float32, jnp.bfloat16
MESH = pl.DeviceIdType.MESH
HIGH = lax.Precision.HIGHEST
TILE = 256
RB = 16


def dot(a, b, dims=((1,), (0,)), precision=None):
    return lax.dot_general(a, b, (dims, ((), ())), preferred_element_type=F32, precision=precision)


def sigmoid(v):
    return jax.nn.sigmoid(v)


def run_all(streams):
    live = list(streams)
    while live:
        for s in list(live):
            try:
                next(s)
            except StopIteration:
                live.remove(s)


def kernel(
    nt, nu, head_count,
    hist, zw, xw, dtw, dtb, alog, cw, cb, dsk, ng, ow, pos, cnt, lab, item, fw, sw,
    enc_o, logit_o, res, g2_o,
    hv, zv, xv, ov, rr, fv, rim, rawf, xb, zb, y, ea, eb, car, sl, st_in, st_out, nb,
    pa, hb, gp, ltb, g, rc, ax_r, ax_l, az_r, az_l, bz_r, bz_l, bx_r, bx_l, s2, s2t, s2u,
    ld_sem, rim_sem, st_sem, pair_sem, rs_sem, ag_sem, s2_sem,
):
    nx = nt // 2
    tm, us = lax.axis_index("tm"), lax.axis_index("user")
    xi, core = tm // 2, tm % 2
    partner = tm + 1 - 2 * core
    rows, width = hist.shape
    inner = zw.shape[1]
    state = (xw.shape[1] - inner) // 2
    head_size = inner // head_count
    slots, hid = item.shape[0], fw.shape[1]
    tiles = inner // TILE
    htiles = hid // TILE

    loads = [
        pltpu.make_async_copy(s, d, ld_sem.at[i])
        for i, (s, d) in enumerate(
            ((hist, hv), (xw, xv), (zw, zv), (fw, fv), (item, rr.at[:, width:]), (ow, ov))
        )
    ]
    for c in loads:
        c.start()

    barrier = pltpu.get_barrier_semaphore()
    for d in range(1, nt):
        pl.semaphore_signal(barrier, inc=1, device_id={"tm": (tm + d) % nt}, device_id_type=MESH)
    for d in range(1, nu):
        pl.semaphore_signal(barrier, inc=1, device_id={"user": (us + d) % nu}, device_id_type=MESH)
    pl.semaphore_wait(barrier, nt + nu - 2)

    def remote(src, dst, ssem, rsem, dev):
        return pltpu.make_async_remote_copy(
            src_ref=src, dst_ref=dst, send_sem=ssem, recv_sem=rsem, device_id=dev, device_id_type=MESH
        )

    loads[0].wait()
    rim_copy = remote(
        hv.at[pl.ds(rows - 16, 16)], rim, rim_sem.at[0], rim_sem.at[1], {"tm": (tm + 1) % nt}
    )

    @pl.when(tm < nt - 1)
    def _():
        rim_copy.start()

    @pl.when(tm == 0)
    def _():
        rim[...] = jnp.zeros_like(rim)
        st_in[...] = jnp.zeros_like(st_in)

    v = dot(hv[...], dtw[...]) + dtb[...]
    dt = jnp.maximum(v, 0.0) + jnp.log1p(jnp.exp(-jnp.abs(v)))
    log_decay = -jnp.exp(alog[...]) * dt
    ri = lax.broadcasted_iota(jnp.int32, (rows, rows), 0)
    ci = lax.broadcasted_iota(jnp.int32, (rows, rows), 1)
    tri = jnp.where(ci <= ri, 1.0, 0.0).astype(F32)
    eye = jnp.where(ci == ri, 1.0, 0.0).astype(F32)
    cum = dot(tri, log_decay, precision=HIGH)
    cum_t = dot(log_decay, tri, ((0,), (1,)), HIGH)
    dt_t = dot(dt, eye, ((0,), (0,)), HIGH)
    eh = lax.broadcasted_iota(jnp.int32, (head_count, inner), 0) * head_size
    ec = lax.broadcasted_iota(jnp.int32, (head_count, inner), 1)
    spread = jnp.where((ec >= eh) & (ec < eh + head_size), 1.0, 0.0).astype(F32)
    last = cum[rows - 1 : rows, :]
    ea[...] = dot(jnp.exp(cum), spread, precision=HIGH)
    eb[...] = dot(jnp.exp(last - cum) * dt, spread, precision=HIGH)
    skip = dot(jnp.broadcast_to(dsk[...], (8, head_count)), spread, precision=HIGH)[0:1]

    loads[1].wait()

    @pl.loop(0, xw.shape[1] // TILE)
    def _(j):
        cols = pl.ds(pl.multiple_of(j * TILE, TILE), TILE)
        rawf[pl.ds(8, rows), cols] = dot(hv[...], xv[:, cols]).astype(BF16).astype(F32)

    @pl.when(tm > 0)
    def _():
        rim_copy.wait_recv()

    @pl.loop(0, xw.shape[1] // TILE)
    def _(j):
        cols = pl.ds(pl.multiple_of(j * TILE, TILE), TILE)
        edge = dot(rim[...], xv[:, cols]).astype(BF16).astype(F32)
        rawf[pl.ds(0, 8), cols] = edge[8:16]
        taps = cw.shape[0]
        acc = jnp.broadcast_to(cb[:, cols], (rows, TILE))
        for k in range(taps):
            acc = acc + cw[pl.ds(k, 1), cols] * rawf[pl.ds(8 - (taps - 1) + k, rows), cols]
        xb[:, cols] = (acc * sigmoid(acc)).astype(BF16)

    b_part = xb[:, inner : inner + state]
    c_part = xb[:, inner + state :]
    for j in range(tiles):
        cols = slice(j * TILE, (j + 1) * TILE)
        car[:, cols] = (eb[:, cols] * xb[:, cols].astype(F32)).astype(BF16)
        sl[j] = dot(b_part, car[:, cols], ((0,), (0,)))

    def st_copy(j):
        return remote(st_out.at[j], st_in.at[j], st_sem.at[0, j], st_sem.at[1, j], {"tm": (tm + 1) % nt})

    def relay():
        for j in range(tiles):
            @pl.when(tm > 0)
            def _():
                st_copy(j).wait_recv()

            @pl.when(tm < nt - 1)
            def _():
                gain = ea[rows - 1 : rows, j * TILE : (j + 1) * TILE]
                st_out[j] = (gain * st_in[j].astype(F32) + sl[j]).astype(BF16)
                st_copy(j).start()

    @pl.when(tm == 0)
    def _():
        relay()

    scores = jnp.where(ci <= ri, dot(c_part, b_part, ((1,), (1,))), 0.0)
    per = 128 // head_size
    lane = lax.broadcasted_iota(jnp.int32, (rows, 128), 1)
    groups = inner // 128
    for q in range(groups):
        xp = xb[:, q * 128 : (q + 1) * 128]
        out = jnp.zeros((rows, 128), F32)
        for r in range(per):
            h = q * per + r
            gap = jnp.minimum(cum[:, h : h + 1] - cum_t[h : h + 1, :], 0.0)
            w = (jnp.exp(gap) * dt_t[h : h + 1, :] * scores).astype(BF16)
            out = jnp.where(lane >= r * head_size, dot(w, xp), out)
        y[:, q * 128 : (q + 1) * 128] = out
        if q == groups // 4:
            @pl.when(tm == 1)
            def _():
                relay()

    loads[2].wait()

    @pl.loop(0, tiles)
    def _(j):
        cols = pl.ds(pl.multiple_of(j * TILE, TILE), TILE)
        zb[:, cols] = dot(hv[...], zv[:, cols]).astype(BF16)

    loads[3].wait()
    loads[4].wait()

    @pl.loop(0, htiles)
    def _(j):
        cols = pl.ds(pl.multiple_of(j * TILE, TILE), TILE)
        pa[:, cols] = dot(rr[:, width:], fv[width:, cols])

    @pl.when(tm > 1)
    def _():
        relay()

    square = jnp.zeros((rows, 1), F32)
    for j in range(tiles):
        cols = slice(j * TILE, (j + 1) * TILE)
        across = ea[:, cols] * dot(c_part, st_in[j])
        zf = zb[:, cols].astype(F32)
        gated = (y[:, cols] + across + skip[:, cols] * xb[:, cols].astype(F32)) * (zf * sigmoid(zf))
        y[:, cols] = gated
        square = square + jnp.sum(gated * gated, axis=1, keepdims=True)
    scale = lax.rsqrt(square / inner + 1e-05)
    for j in range(tiles):
        cols = slice(j * TILE, (j + 1) * TILE)
        nb[:, cols] = (y[:, cols] * scale * ng[:, cols]).astype(BF16)
    loads[5].wait()

    @pl.loop(0, width // TILE)
    def _(j):
        cols = pl.ds(pl.multiple_of(j * TILE, TILE), TILE)
        enc_o[:, cols] = dot(nb[...], ov[:, cols]).astype(BF16)

    local = pos[...] - tm * rows
    pick = lax.broadcasted_iota(jnp.int32, (rows, slots), 0) == local
    pick = jnp.where(pick, 1.0, 0.0).astype(BF16)
    rr[:, :width] = dot(pick, enc_o[...], ((0,), (0,))).astype(BF16)

    @pl.loop(0, htiles)
    def _(j):
        cols = pl.ds(pl.multiple_of(j * TILE, TILE), TILE)
        p = pa[:, cols] + dot(rr[:, :width], fv[:width, cols])
        pa[:, cols] = p
        hb[:, cols] = (p * sigmoid(p)).astype(BF16)

    logit = dot(jnp.broadcast_to(sw[...], (16, hid)), hb[...], ((1,), (1,)))[0:1]
    live = (lax.broadcasted_iota(jnp.int32, (1, slots), 1) < cnt[...]).astype(F32)
    logit_o[...] = live * logit
    dl = live * (sigmoid(logit) - lab[...].astype(F32))
    d1 = dl.astype(BF16).astype(F32)
    d2 = (dl - d1).astype(BF16).astype(F32)
    d3 = dl - d1 - d2
    ki = lax.broadcasted_iota(jnp.int32, (16, slots), 0)
    lhs = jnp.where(ki == 0, d1, jnp.where(ki == 1, d2, jnp.where(ki == 2, d3, 0.0))).astype(BF16)
    second = jnp.sum(dot(lhs, hb[...]), axis=0, keepdims=True)
    for j in range(hid // 128):
        s2[j : j + 1, :] = second[:, j * 128 : (j + 1) * 128]
    s2_copies = [
        remote(s2, s2t.at[d - 1], s2_sem.at[0, d - 1], s2_sem.at[1, d - 1], {"tm": (tm + d) % nt})
        for d in range(1, nt)
    ]
    for c in s2_copies:
        c.start()

    dcol = jnp.transpose(jnp.broadcast_to(dl, (128, slots)))
    dcol = jnp.concatenate([dcol] * (TILE // 128), axis=1)

    @pl.loop(0, htiles)
    def _(j):
        cols = pl.ds(pl.multiple_of(j * TILE, TILE), TILE)
        p = pa[:, cols]
        sig = sigmoid(p)
        gp[:, cols] = (dcol * sw[:, cols].astype(F32) * (sig * (1.0 + p * (1.0 - sig)))).astype(BF16)

    blocks = g.shape[0]
    half, part = blocks // 2, blocks // 4
    mine = core * half
    other = half - mine
    prow = part // htiles * RB

    def pair_copy(k):
        return remote(
            g.at[pl.ds(other + k * part, part)], rc.at[pl.ds(k * part, part)],
            pair_sem.at[0, k], pair_sem.at[1, k], {"tm": partner},
        )

    for k in range(4):
        first = (other if k < 2 else mine) + (k % 2) * part
        r0 = pl.multiple_of(first // htiles * RB, 128)
        for m in range(prow // TILE):
            ltb[...] = jnp.transpose(rr[:, pl.ds(r0 + m * TILE, TILE)])

            @pl.loop(0, htiles)
            def _(j):
                cols = pl.ds(pl.multiple_of(j * TILE, TILE), TILE)
                out = dot(ltb[...], gp[:, cols]).astype(BF16)
                for i in range(TILE // RB):
                    g[first + (m * (TILE // RB) + i) * htiles + j] = out[i * RB : (i + 1) * RB]

        if k < 2:
            pair_copy(k).start()

    def add(dst, dst0, a, a0, b, b0, count):
        step = min(count, 8)

        @pl.loop(0, count // step)
        def _(i):
            o = i * step
            dst[pl.ds(dst0 + o, step)] = (
                a[pl.ds(a0 + o, step)].astype(F32) + b[pl.ds(b0 + o, step)].astype(F32)
            ).astype(BF16)

    def rs(axis, me, n, base, share, right, left, sid, final):
        def dev(p):
            return {"tm": 2 * p + core} if axis == "x" else {"user": p}

        up, down = (me + 1) % n, (me + n - 1) % n

        def to_right(d):
            return remote(
                g.at[pl.ds(base + (me + d) * share, share)], right.at[pl.ds((d - 1) * share, share)],
                rs_sem.at[sid, 0, d], rs_sem.at[sid, 1, d - 1], dev(up),
            )

        def to_left(d):
            return remote(
                g.at[pl.ds(base + (me - d) * share, share)], left.at[pl.ds((d - 1) * share, share)],
                rs_sem.at[sid, 2, d], rs_sem.at[sid, 3, d - 1], dev(down),
            )

        def got(buf, d, lane_id):
            slot = buf.at[pl.ds(d * share, share)]
            remote(slot, slot, rs_sem.at[sid, lane_id - 1, d], rs_sem.at[sid, lane_id, d], dev(up)).wait_recv()

        for d in range(n - 1, 0, -1):
            @pl.when(me + d < n)
            def _():
                if d < n - 1:
                    @pl.when(me > 0)
                    def _():
                        got(right, d, 1)
                        s = base + (me + d) * share
                        add(g, s, g, s, right, d * share, share)
                to_right(d).start()

            @pl.when(me - d >= 0)
            def _():
                if d < n - 1:
                    @pl.when(me < n - 1)
                    def _():
                        got(left, d, 3)
                        s = base + (me - d) * share
                        add(g, s, g, s, left, d * share, share)
                to_left(d).start()
            yield
        own = base + me * share

        @pl.when(me > 0)
        def _():
            got(right, 0, 1)
            add(g, own, g, own, right, 0, share)

        @pl.when(me < n - 1)
        def _():
            got(left, 0, 3)
            add(g, own, g, own, left, 0, share)

        if final:
            res[pl.ds(own, share)] = g[pl.ds(own, share)]
        for d in range(n - 1, 0, -1):
            @pl.when(me + d < n)
            def _():
                to_right(d).wait_send()

            @pl.when(me - d >= 0)
            def _():
                to_left(d).wait_send()
        yield

    def ag(axis, me, n, base, share, sid):
        def dev(p):
            return {"tm": 2 * p + core} if axis == "x" else {"user": p}

        up, down = (me + 1) % n, (me + n - 1) % n

        def move(d, way):
            spot = res.at[pl.ds(base + (me - way * d) * share, share)]
            k = 0 if way > 0 else 2
            return remote(
                spot, spot, ag_sem.at[sid, k, d], ag_sem.at[sid, k + 1, d + 1], dev(up if way > 0 else down)
            )

        def got(d, way):
            spot = res.at[pl.ds(base + (me - way * d) * share, share)]
            k = 0 if way > 0 else 2
            remote(spot, spot, ag_sem.at[sid, k, d], ag_sem.at[sid, k + 1, d], dev(up)).wait_recv()

        for d in range(n):
            @pl.when(me - d >= 0)
            def _():
                if d:
                    got(d, 1)

                if d < n - 1:
                    @pl.when(me < n - 1)
                    def _():
                        move(d, 1).start()

            @pl.when(me + d < n)
            def _():
                if d:
                    got(d, -1)

                if d < n - 1:
                    @pl.when(me > 0)
                    def _():
                        move(d, -1).start()
            yield
        for d in range(n - 1):
            @pl.when((me - d >= 0) & (me < n - 1))
            def _():
                move(d, 1).wait_send()

            @pl.when((me + d < n) & (me > 0))
            def _():
                move(d, -1).wait_send()

    def finish(base, k):
        spot = res.at[pl.ds(base, part)]
        return remote(spot, spot, pair_sem.at[0, 2 + k], pair_sem.at[1, 2 + k], {"tm": partner})

    def stream_a():
        pair_copy(0).wait_recv()
        add(g, mine, g, mine, rc, 0, part)
        sx = part // nx
        sz = sx // nu
        xbase = mine + xi * sx
        yield from rs("x", xi, nx, mine, sx, ax_r, ax_l, 0, False)
        yield from rs("z", us, nu, xbase, sz, az_r, az_l, 1, True)
        yield from ag("z", us, nu, xbase, sz, 0)
        yield from ag("x", xi, nx, mine, sx, 1)
        finish(mine, 0).start()

    def stream_b():
        pair_copy(1).wait_recv()
        base = mine + part
        add(g, base, g, base, rc, part, part)
        sz = part // nu
        sx = sz // nx
        zbase = base + us * sz
        yield from rs("z", us, nu, base, sz, bz_r, bz_l, 2, False)
        yield from rs("x", xi, nx, zbase, sx, bx_r, bx_l, 3, True)
        yield from ag("x", xi, nx, zbase, sx, 2)
        yield from ag("z", us, nu, base, sz, 3)
        finish(base, 1).start()

    def stream_c():
        yield
        for c in s2_copies:
            c.wait_recv()
        total = s2[...]
        for d in range(nt - 1):
            total = total + s2t[d]
        for c in s2_copies:
            c.wait_send()
        s2[...] = total
        more = [
            remote(s2, s2u.at[d - 1], s2_sem.at[2, d - 1], s2_sem.at[3, d - 1], {"user": (us + d) % nu})
            for d in range(1, nu)
        ]
        for c in more:
            c.start()
        for _ in range(3):
            yield
        for c in more:
            c.wait_recv()
        for d in range(nu - 1):
            total = total + s2u[d]
        g2_o[...] = total
        for c in more:
            c.wait_send()

    run_all([stream_a(), stream_b(), stream_c()])
    for k in range(2):
        spot = res.at[pl.ds(other + k * part, part)]
        remote(spot, spot, pair_sem.at[0, 2 + k], pair_sem.at[1, 2 + k], {"tm": partner}).wait_recv()
        finish(mine + k * part, k).wait_send()
        pair_copy(k).wait_send()

    @pl.when(tm < nt - 1)
    def _():
        rim_copy.wait_send()
        for j in range(tiles):
            st_copy(j).wait_send()


def widen(blocks_ref, out_ref):
    htiles = out_ref.shape[1] // TILE
    for b in range(blocks_ref.shape[0]):
        r, c = b // htiles * RB, b % htiles * TILE
        out_ref[r : r + RB, c : c + TILE] = blocks_ref[b].astype(F32)


def body(nt, nu, history, z_weight, xbc_weight, dt_weight, dt_bias, a_log, conv_weight, conv_bias,
         d_skip, norm_gain, out_weight, label_pos, label_count, label_value, item_feat,
         first_weight, second_weight):
    rows, width = history.shape[1:]
    inner, xbc = z_weight.shape[1], xbc_weight.shape[1]
    state = (xbc - inner) // 2
    heads = a_log.shape[0]
    slots = item_feat.shape[1]
    fan, hid = first_weight.shape
    tiles = inner // TILE
    blocks = fan * hid // (RB * TILE)
    part = blocks // 4
    nx = nt // 2
    most = max(nt, nu)

    def vm(shape, dtype=BF16):
        return pltpu.VMEM(shape, dtype)

    slab = (part, RB, TILE)
    scratch = [
        vm((rows, width)), vm((width, inner)), vm((width, xbc)), vm((inner, width)),
        vm((slots, fan)), vm((fan, hid)), vm((16, width)), vm((rows + 8, xbc), F32),
        vm((rows, xbc)), vm((rows, inner)), vm((rows, inner), F32), vm((rows, inner), F32),
        vm((rows, inner), F32), vm((rows, inner)), vm((tiles, state, TILE), F32),
        vm((tiles, state, TILE)), vm((tiles, state, TILE)), vm((rows, inner)),
        vm((slots, hid), F32), vm((slots, hid)), vm((slots, hid)), vm((TILE, slots)),
        vm((blocks, RB, TILE)), vm((blocks // 2, RB, TILE)),
        vm(slab), vm(slab), vm((part // nx, RB, TILE)), vm((part // nx, RB, TILE)),
        vm(slab), vm(slab), vm((part // nu, RB, TILE)), vm((part // nu, RB, TILE)),
        vm((hid // 128, 128), F32), vm((nt - 1, hid // 128, 128), F32), vm((nu - 1, hid // 128, 128), F32),
        pltpu.SemaphoreType.DMA((6,)), pltpu.SemaphoreType.DMA((2,)), pltpu.SemaphoreType.DMA((2, tiles)),
        pltpu.SemaphoreType.DMA((2, 4)), pltpu.SemaphoreType.DMA((4, 4, most)),
        pltpu.SemaphoreType.DMA((4, 4, most + 1)), pltpu.SemaphoreType.DMA((4, most)),
    ]
    hbm, vmem = pl.BlockSpec(memory_space=pl.ANY), pl.BlockSpec(memory_space=pltpu.VMEM)
    enc, logit, grads, second = pl.pallas_call(
        functools.partial(kernel, nt, nu, heads),
        out_shape=(
            jax.ShapeDtypeStruct((rows, width), BF16),
            jax.ShapeDtypeStruct((1, slots), F32),
            jax.ShapeDtypeStruct((blocks, RB, TILE), BF16),
            jax.ShapeDtypeStruct((hid // 128, 128), F32),
        ),
        in_specs=[hbm, hbm, hbm] + [vmem] * 7 + [hbm] + [vmem] * 3 + [hbm, hbm, vmem],
        out_specs=(vmem, vmem, vmem, vmem),
        scratch_shapes=scratch,
        compiler_params=pltpu.CompilerParams(
            collective_id=0, has_side_effects=True, vmem_limit_bytes=56 * 1024 * 1024
        ),
    )(
        history[0], z_weight, xbc_weight, dt_weight, dt_bias[None], a_log[None], conv_weight,
        conv_bias[None], d_skip[None], norm_gain[None], out_weight, label_pos, label_count,
        label_value, item_feat[0], first_weight, second_weight[None],
    )
    steps = 8
    wide = pl.pallas_call(
        widen,
        grid=(steps,),
        out_shape=jax.ShapeDtypeStruct((fan, hid), F32),
        in_specs=[pl.BlockSpec((blocks // steps, RB, TILE), lambda i: (i, 0, 0))],
        out_specs=pl.BlockSpec((fan // steps, hid), lambda i: (i, 0)),
    )(grads)
    return enc[None], logit, wide, second.reshape(hid)


def solution(mesh):
    row = P(("grp", "user"), "tm", None)
    row2 = P(("grp", "user"), "tm")
    in_specs = (row,) + (P(),) * 10 + (row2, row2, row2, row, P(), P())
    out_specs = (row, row2, P("grp", None), P("grp"))
    return jax.shard_map(
        functools.partial(body, mesh.shape["tm"], mesh.shape["user"]),
        mesh=mesh, in_specs=in_specs, out_specs=out_specs, check_vma=False,
    )
```

```python
import functools

import jax
import jax.numpy as jnp
from jax import lax
from jax.experimental import pallas as pl
from jax.experimental.pallas import tpu as pltpu
from jax.sharding import PartitionSpec as P

F32, BF16 = jnp.float32, jnp.bfloat16
MESH = pl.DeviceIdType.MESH
HIGH = lax.Precision.HIGHEST
TILE = 256
RB = 16


def dot(a, b, dims=((1,), (0,)), precision=None):
    return lax.dot_general(a, b, (dims, ((), ())), preferred_element_type=F32, precision=precision)


def sigmoid(v):
    return jax.nn.sigmoid(v)


def advance(stream, steps):
    for _ in range(steps):
        next(stream, None)


def kernel(
    nt, nu, head_count,
    hist, zw, xw, dtw, dtb, alog, cw, cb, dsk, ng, ow, pos, cnt, lab, item, fw, sw,
    enc_o, logit_o, res, g2_o,
    hv, zv, xv, ov, rr, fv, rim, rawf, xb, zb, y, ea, eb, car, sl, st_in, st_out, nb,
    pa, hb, gp, ltb, g, rc, ax_r, ax_l, az_r, az_l, bz_r, bz_l, bx_r, bx_l, s2, s2t, s2u,
    ld_sem, rim_sem, st_sem, pair_sem, rs_sem, ag_sem, s2_sem,
):
    nx = nt // 2
    tm, us = lax.axis_index("tm"), lax.axis_index("user")
    xi, core = tm // 2, tm % 2
    partner = tm + 1 - 2 * core
    rows, width = hist.shape
    inner = zw.shape[1]
    state = (xw.shape[1] - inner) // 2
    head_size = inner // head_count
    slots, hid = item.shape[0], fw.shape[1]
    tiles = inner // TILE
    htiles = hid // TILE

    loads = [
        pltpu.make_async_copy(s, d, ld_sem.at[i])
        for i, (s, d) in enumerate(
            ((hist, hv), (xw, xv), (zw, zv), (fw, fv), (item, rr.at[:, width:]), (ow, ov))
        )
    ]
    for c in loads:
        c.start()

    barrier = pltpu.get_barrier_semaphore()
    for d in range(1, nt):
        pl.semaphore_signal(barrier, inc=1, device_id={"tm": (tm + d) % nt}, device_id_type=MESH)
    for d in range(1, nu):
        pl.semaphore_signal(barrier, inc=1, device_id={"user": (us + d) % nu}, device_id_type=MESH)
    pl.semaphore_wait(barrier, nt + nu - 2)

    def remote(src, dst, ssem, rsem, dev):
        return pltpu.make_async_remote_copy(
            src_ref=src, dst_ref=dst, send_sem=ssem, recv_sem=rsem, device_id=dev, device_id_type=MESH
        )

    loads[0].wait()
    rim_copy = remote(
        hv.at[pl.ds(rows - 16, 16)], rim, rim_sem.at[0], rim_sem.at[1], {"tm": (tm + 1) % nt}
    )

    @pl.when(tm < nt - 1)
    def _():
        rim_copy.start()

    @pl.when(tm == 0)
    def _():
        rim[...] = jnp.zeros_like(rim)
        st_in[...] = jnp.zeros_like(st_in)

    v = dot(hv[...], dtw[...], ((1,), (1,))) + dtb[...].reshape(1, head_count)
    dt = jnp.maximum(v, 0.0) + jnp.log1p(jnp.exp(-jnp.abs(v)))
    log_decay = -jnp.exp(alog[...].reshape(1, head_count)) * dt
    ri = lax.broadcasted_iota(jnp.int32, (rows, rows), 0)
    ci = lax.broadcasted_iota(jnp.int32, (rows, rows), 1)
    tri = jnp.where(ci <= ri, 1.0, 0.0).astype(F32)
    eye = jnp.where(ci == ri, 1.0, 0.0).astype(F32)
    cum = dot(tri, log_decay, precision=HIGH)
    cum_t = dot(log_decay, tri, ((0,), (1,)), HIGH)
    dt_t = dot(dt, eye, ((0,), (0,)), HIGH)
    eh = lax.broadcasted_iota(jnp.int32, (head_count, inner), 0) * head_size
    ec = lax.broadcasted_iota(jnp.int32, (head_count, inner), 1)
    spread = jnp.where((ec >= eh) & (ec < eh + head_size), 1.0, 0.0).astype(F32)
    last = cum[rows - 1 : rows, :]
    ea[...] = dot(jnp.exp(cum), spread, precision=HIGH)
    eb[...] = dot(jnp.exp(last - cum) * dt, spread, precision=HIGH)
    skip = dot(jnp.broadcast_to(dsk[...].reshape(1, head_count), (8, head_count)), spread, precision=HIGH)[0:1]

    loads[1].wait()

    @pl.loop(0, xw.shape[1] // TILE)
    def _(j):
        cols = pl.ds(pl.multiple_of(j * TILE, TILE), TILE)
        rawf[pl.ds(8, rows), cols] = dot(hv[...], xv[:, cols]).astype(BF16).astype(F32)

    @pl.when(tm > 0)
    def _():
        rim_copy.wait_recv()

    @pl.loop(0, xw.shape[1] // TILE)
    def _(j):
        cols = pl.ds(pl.multiple_of(j * TILE, TILE), TILE)
        edge = dot(rim[...], xv[:, cols]).astype(BF16).astype(F32)
        rawf[pl.ds(0, 8), cols] = edge[8:16]
        taps = cw.shape[0]
        acc = jnp.broadcast_to(cb[cols].reshape(1, TILE), (rows, TILE))
        for k in range(taps):
            acc = acc + cw[pl.ds(k, 1), cols] * rawf[pl.ds(8 - (taps - 1) + k, rows), cols]
        xb[:, cols] = (acc * sigmoid(acc)).astype(BF16)

    b_part = xb[:, inner : inner + state]
    c_part = xb[:, inner + state :]
    for j in range(tiles):
        cols = slice(j * TILE, (j + 1) * TILE)
        car[:, cols] = (eb[:, cols] * xb[:, cols].astype(F32)).astype(BF16)
        sl[j] = dot(b_part, car[:, cols], ((0,), (0,)))

    def st_copy(j):
        return remote(st_out.at[j], st_in.at[j], st_sem.at[0, j], st_sem.at[1, j], {"tm": (tm + 1) % nt})

    def relay():
        for j in range(tiles):
            @pl.when(tm > 0)
            def _():
                st_copy(j).wait_recv()

            @pl.when(tm < nt - 1)
            def _():
                gain = ea[rows - 1 : rows, j * TILE : (j + 1) * TILE]
                st_out[j] = (gain * st_in[j].astype(F32) + sl[j]).astype(BF16)
                st_copy(j).start()

    @pl.when(tm == 0)
    def _():
        relay()

    scores = jnp.where(ci <= ri, dot(c_part, b_part, ((1,), (1,))), 0.0)
    per = 128 // head_size
    lane = lax.broadcasted_iota(jnp.int32, (rows, 128), 1)
    groups = inner // 128
    for q in range(groups):
        xp = xb[:, q * 128 : (q + 1) * 128]
        out = jnp.zeros((rows, 128), F32)
        for r in range(per):
            h = q * per + r
            gap = jnp.minimum(cum[:, h : h + 1] - cum_t[h : h + 1, :], 0.0)
            w = (jnp.exp(gap) * dt_t[h : h + 1, :] * scores).astype(BF16)
            out = jnp.where(lane >= r * head_size, dot(w, xp), out)
        y[:, q * 128 : (q + 1) * 128] = out
        if q == groups // 4:
            @pl.when(tm == 1)
            def _():
                relay()

    loads[2].wait()

    @pl.loop(0, tiles)
    def _(j):
        cols = pl.ds(pl.multiple_of(j * TILE, TILE), TILE)
        zb[:, cols] = dot(hv[...], zv[:, cols]).astype(BF16)

    loads[3].wait()
    loads[4].wait()

    @pl.loop(0, htiles)
    def _(j):
        cols = pl.ds(pl.multiple_of(j * TILE, TILE), TILE)
        pa[:, cols] = dot(rr[:, width:], fv[width:, cols])

    @pl.when(tm > 1)
    def _():
        relay()

    square = jnp.zeros((rows, 1), F32)
    for j in range(tiles):
        cols = slice(j * TILE, (j + 1) * TILE)
        across = ea[:, cols] * dot(c_part, st_in[j])
        zf = zb[:, cols].astype(F32)
        gated = (y[:, cols] + across + skip[:, cols] * xb[:, cols].astype(F32)) * (zf * sigmoid(zf))
        y[:, cols] = gated
        square = square + jnp.sum(gated * gated, axis=1, keepdims=True)
    scale = lax.rsqrt(square / inner + 1e-05)
    for j in range(tiles):
        cols = slice(j * TILE, (j + 1) * TILE)
        nb[:, cols] = (y[:, cols] * scale * ng[cols].reshape(1, TILE)).astype(BF16)
    loads[5].wait()

    @pl.loop(0, width // TILE)
    def _(j):
        cols = pl.ds(pl.multiple_of(j * TILE, TILE), TILE)
        enc_o[:, cols] = dot(nb[...], ov[:, cols]).astype(BF16)

    local = pos[...] - tm * rows
    pick = lax.broadcasted_iota(jnp.int32, (rows, slots), 0) == local
    pick = jnp.where(pick, 1.0, 0.0).astype(BF16)
    rr[:, :width] = dot(pick, enc_o[...], ((0,), (0,))).astype(BF16)

    @pl.loop(0, htiles)
    def _(j):
        cols = pl.ds(pl.multiple_of(j * TILE, TILE), TILE)
        p = pa[:, cols] + dot(rr[:, :width], fv[:width, cols])
        pa[:, cols] = p
        hb[:, cols] = (p * sigmoid(p)).astype(BF16)

    logit = dot(jnp.broadcast_to(sw[...].astype(F32).reshape(1, hid), (16, hid)).astype(BF16), hb[...], ((1,), (1,)))[0:1]
    live = (lax.broadcasted_iota(jnp.int32, (1, slots), 1) < cnt[...]).astype(F32)
    logit_o[...] = live * logit
    dl = live * (sigmoid(logit) - lab[...].astype(F32))
    d1 = dl.astype(BF16).astype(F32)
    d2 = (dl - d1).astype(BF16).astype(F32)
    d3 = dl - d1 - d2
    ki = lax.broadcasted_iota(jnp.int32, (16, slots), 0)
    lhs = jnp.where(ki == 0, d1, jnp.where(ki == 1, d2, jnp.where(ki == 2, d3, 0.0))).astype(BF16)
    second = jnp.sum(dot(lhs, hb[...]), axis=0, keepdims=True)
    for j in range(hid // 128):
        s2[j : j + 1, :] = second[:, j * 128 : (j + 1) * 128]
    s2_copies = [
        remote(s2, s2t.at[d - 1], s2_sem.at[0, d - 1], s2_sem.at[1, d - 1], {"tm": (tm + d) % nt})
        for d in range(1, nt)
    ]
    for c in s2_copies:
        c.start()

    dcol = jnp.transpose(jnp.broadcast_to(dl, (128, slots)))
    dcol = jnp.concatenate([dcol] * (TILE // 128), axis=1)

    @pl.loop(0, htiles)
    def _(j):
        cols = pl.ds(pl.multiple_of(j * TILE, TILE), TILE)
        p = pa[:, cols]
        sig = sigmoid(p)
        gp[:, cols] = (dcol * sw[cols].astype(F32).reshape(1, TILE) * (sig * (1.0 + p * (1.0 - sig)))).astype(BF16)

    blocks = g.shape[0]
    half, part = blocks // 2, blocks // 4
    mine = core * half
    other = half - mine
    prow = part // htiles * RB

    def pair_copy(k):
        return remote(
            g.at[pl.ds(other + k * part, part)], rc.at[pl.ds(k * part, part)],
            pair_sem.at[0, k], pair_sem.at[1, k], {"tm": partner},
        )

    for k in range(4):
        first = (other if k < 2 else mine) + (k % 2) * part
        r0 = pl.multiple_of(first // htiles * RB, 128)
        for m in range(prow // TILE):
            ltb[...] = jnp.transpose(rr[:, pl.ds(r0 + m * TILE, TILE)])

            @pl.loop(0, htiles)
            def _(j):
                cols = pl.ds(pl.multiple_of(j * TILE, TILE), TILE)
                out = dot(ltb[...], gp[:, cols]).astype(BF16)
                for i in range(TILE // RB):
                    g[first + (m * (TILE // RB) + i) * htiles + j] = out[i * RB : (i + 1) * RB]

        if k < 2:
            pair_copy(k).start()

    def add(dst, dst0, a, a0, b, b0, count):
        step = min(count, 8)

        @pl.loop(0, count // step)
        def _(i):
            o = i * step
            dst[pl.ds(dst0 + o, step)] = (
                a[pl.ds(a0 + o, step)].astype(F32) + b[pl.ds(b0 + o, step)].astype(F32)
            ).astype(BF16)

    later = []

    def rs(axis, me, n, base, share, right, left, sid, final):
        def dev(p):
            return {"tm": 2 * p + core} if axis == "x" else {"user": p}

        up, down = (me + 1) % n, (me + n - 1) % n

        def to_right(d):
            return remote(
                g.at[pl.ds(base + (me + d) * share, share)], right.at[pl.ds((d - 1) * share, share)],
                rs_sem.at[sid, 0, d], rs_sem.at[sid, 1, d - 1], dev(up),
            )

        def to_left(d):
            return remote(
                g.at[pl.ds(base + (me - d) * share, share)], left.at[pl.ds((d - 1) * share, share)],
                rs_sem.at[sid, 2, d], rs_sem.at[sid, 3, d - 1], dev(down),
            )

        def got(buf, d, lane_id):
            slot = buf.at[pl.ds(d * share, share)]
            remote(slot, slot, rs_sem.at[sid, lane_id - 1, d], rs_sem.at[sid, lane_id, d], dev(up)).wait_recv()

        for d in range(n - 1, 0, -1):
            @pl.when(me + d < n)
            def _():
                if d < n - 1:
                    @pl.when(me > 0)
                    def _():
                        got(right, d, 1)
                        s = base + (me + d) * share
                        add(g, s, g, s, right, d * share, share)
                to_right(d).start()

            @pl.when(me - d >= 0)
            def _():
                if d < n - 1:
                    @pl.when(me < n - 1)
                    def _():
                        got(left, d, 3)
                        s = base + (me - d) * share
                        add(g, s, g, s, left, d * share, share)
                to_left(d).start()
            yield
        own = base + me * share

        @pl.when(me > 0)
        def _():
            got(right, 0, 1)
            add(g, own, g, own, right, 0, share)

        @pl.when(me < n - 1)
        def _():
            got(left, 0, 3)
            add(g, own, g, own, left, 0, share)

        if final:
            res[pl.ds(own, share)] = g[pl.ds(own, share)]

        def drain():
            for d in range(n - 1, 0, -1):
                @pl.when(me + d < n)
                def _():
                    to_right(d).wait_send()

                @pl.when(me - d >= 0)
                def _():
                    to_left(d).wait_send()

        later.append(drain)
        yield

    def ag(axis, me, n, base, share, sid):
        def dev(p):
            return {"tm": 2 * p + core} if axis == "x" else {"user": p}

        up, down = (me + 1) % n, (me + n - 1) % n

        def move(d, way):
            spot = res.at[pl.ds(base + (me - way * d) * share, share)]
            k = 0 if way > 0 else 2
            return remote(
                spot, spot, ag_sem.at[sid, k, d], ag_sem.at[sid, k + 1, d + 1], dev(up if way > 0 else down)
            )

        def got(d, way):
            spot = res.at[pl.ds(base + (me - way * d) * share, share)]
            k = 0 if way > 0 else 2
            remote(spot, spot, ag_sem.at[sid, k, d], ag_sem.at[sid, k + 1, d], dev(up)).wait_recv()

        for d in range(n):
            @pl.when(me - d >= 0)
            def _():
                if d:
                    got(d, 1)

                if d < n - 1:
                    @pl.when(me < n - 1)
                    def _():
                        move(d, 1).start()

            @pl.when(me + d < n)
            def _():
                if d:
                    got(d, -1)

                if d < n - 1:
                    @pl.when(me > 0)
                    def _():
                        move(d, -1).start()
            yield

        def drain():
            for d in range(n - 1):
                @pl.when((me - d >= 0) & (me < n - 1))
                def _():
                    move(d, 1).wait_send()

                @pl.when((me + d < n) & (me > 0))
                def _():
                    move(d, -1).wait_send()

        later.append(drain)

    def finish(base, k):
        spot = res.at[pl.ds(base, part)]
        return remote(spot, spot, pair_sem.at[0, 2 + k], pair_sem.at[1, 2 + k], {"tm": partner})

    def stream_a():
        pair_copy(0).wait_recv()
        add(g, mine, g, mine, rc, 0, part)
        sx = part // nx
        sz = sx // nu
        xbase = mine + xi * sx
        yield from rs("x", xi, nx, mine, sx, ax_r, ax_l, 0, False)
        yield from rs("z", us, nu, xbase, sz, az_r, az_l, 1, True)
        yield from ag("z", us, nu, xbase, sz, 0)
        yield from ag("x", xi, nx, mine, sx, 1)
        finish(mine, 0).start()

    def stream_b():
        pair_copy(1).wait_recv()
        base = mine + part
        add(g, base, g, base, rc, part, part)
        sz = part // nu
        sx = sz // nx
        zbase = base + us * sz
        yield from rs("z", us, nu, base, sz, bz_r, bz_l, 2, False)
        yield from rs("x", xi, nx, zbase, sx, bx_r, bx_l, 3, True)
        yield from ag("x", xi, nx, zbase, sx, 2)
        yield from ag("z", us, nu, base, sz, 3)
        finish(base, 1).start()

    def stream_c():
        for c in s2_copies:
            c.wait_recv()
        total = s2[...]
        for d in range(nt - 1):
            total = total + s2t[d]
        for c in s2_copies:
            c.wait_send()
        s2[...] = total
        more = [
            remote(s2, s2u.at[d - 1], s2_sem.at[2, d - 1], s2_sem.at[3, d - 1], {"user": (us + d) % nu})
            for d in range(1, nu)
        ]
        for c in more:
            c.start()
        yield
        for c in more:
            c.wait_recv()
        for d in range(nu - 1):
            total = total + s2u[d]
        g2_o[...] = total
        for c in more:
            c.wait_send()

    sa, sb, sc = stream_a(), stream_b(), stream_c()
    advance(sa, nx - 1)
    advance(sb, nu)
    advance(sa, 1)
    advance(sb, nx - 1)
    advance(sa, nu)
    advance(sc, 1)
    advance(sb, 2)
    advance(sa, nu)
    advance(sb, nx - 1)
    advance(sa, 1)
    advance(sb, nu)
    advance(sa, nx)
    advance(sb, 1)
    advance(sc, 1)
    for drain in later:
        drain()
    for k in range(2):
        spot = res.at[pl.ds(other + k * part, part)]
        remote(spot, spot, pair_sem.at[0, 2 + k], pair_sem.at[1, 2 + k], {"tm": partner}).wait_recv()
        finish(mine + k * part, k).wait_send()
        pair_copy(k).wait_send()

    @pl.when(tm < nt - 1)
    def _():
        rim_copy.wait_send()
        for j in range(tiles):
            st_copy(j).wait_send()


def widen(chunks, enc, logit, second, grads, enc_o, logit_o, second_o, wide_o, held, wide, in_sem, out_sem):
    blocks, rows = grads.shape[0] // chunks, wide_o.shape[0] // chunks
    htiles = wide_o.shape[1] // TILE
    small = [
        pltpu.make_async_copy(a, b, out_sem.at[chunks + i])
        for i, (a, b) in enumerate(((enc, enc_o), (logit, logit_o), (second, second_o)))
    ]
    ins = [
        pltpu.make_async_copy(grads.at[pl.ds(k * blocks, blocks)], held.at[k], in_sem.at[k])
        for k in range(chunks)
    ]
    outs = [
        pltpu.make_async_copy(wide.at[k], wide_o.at[pl.ds(k * rows, rows)], out_sem.at[k])
        for k in range(chunks)
    ]
    for c in ins + small:
        c.start()
    for k in range(chunks):
        ins[k].wait()
        for b in range(blocks):
            r, c = b // htiles * RB, b % htiles * TILE
            wide[k, r : r + RB, c : c + TILE] = held[k, b].astype(F32)
        outs[k].start()
    for c in outs + small:
        c.wait()


def body(nt, nu, history, z_weight, xbc_weight, dt_weight, dt_bias, a_log, conv_weight, conv_bias,
         d_skip, norm_gain, out_weight, label_pos, label_count, label_value, item_feat,
         first_weight, second_weight):
    rows, width = history.shape[1:]
    inner, xbc = z_weight.shape[1], xbc_weight.shape[1]
    state = (xbc - inner) // 2
    heads = a_log.shape[0]
    slots = item_feat.shape[1]
    fan, hid = first_weight.shape
    tiles = inner // TILE
    blocks = fan * hid // (RB * TILE)
    part = blocks // 4
    nx = nt // 2
    most = max(nt, nu)

    def vm(shape, dtype=BF16):
        return pltpu.VMEM(shape, dtype)

    slab = (part, RB, TILE)
    scratch = [
        vm((rows, width)), vm((width, inner)), vm((width, xbc)), vm((inner, width)),
        vm((slots, fan)), vm((fan, hid)), vm((16, width)), vm((rows + 8, xbc), F32),
        vm((rows, xbc)), vm((rows, inner)), vm((rows, inner), F32), vm((rows, inner), F32),
        vm((rows, inner), F32), vm((rows, inner)), vm((tiles, state, TILE), F32),
        vm((tiles, state, TILE)), vm((tiles, state, TILE)), vm((rows, inner)),
        vm((slots, hid), F32), vm((slots, hid)), vm((slots, hid)), vm((TILE, slots)),
        vm((blocks, RB, TILE)), vm((blocks // 2, RB, TILE)),
        vm(slab), vm(slab), vm((part // nx, RB, TILE)), vm((part // nx, RB, TILE)),
        vm(slab), vm(slab), vm((part // nu, RB, TILE)), vm((part // nu, RB, TILE)),
        vm((hid // 128, 128), F32), vm((nt - 1, hid // 128, 128), F32), vm((nu - 1, hid // 128, 128), F32),
        pltpu.SemaphoreType.DMA((6,)), pltpu.SemaphoreType.DMA((2,)), pltpu.SemaphoreType.DMA((2, tiles)),
        pltpu.SemaphoreType.DMA((2, 4)), pltpu.SemaphoreType.DMA((4, 4, most)),
        pltpu.SemaphoreType.DMA((4, 4, most + 1)), pltpu.SemaphoreType.DMA((4, most)),
    ]
    hbm, vmem = pl.BlockSpec(memory_space=pl.ANY), pl.BlockSpec(memory_space=pltpu.VMEM)
    enc, logit, grads, second = pl.pallas_call(
        functools.partial(kernel, nt, nu, heads),
        out_shape=(
            jax.ShapeDtypeStruct((rows, width), BF16),
            jax.ShapeDtypeStruct((1, slots), F32),
            jax.ShapeDtypeStruct((blocks, RB, TILE), BF16),
            jax.ShapeDtypeStruct((hid // 128, 128), F32),
        ),
        in_specs=[hbm, hbm, hbm] + [vmem] * 7 + [hbm] + [vmem] * 3 + [hbm, hbm, vmem],
        out_specs=(vmem, vmem, vmem, vmem),
        scratch_shapes=scratch,
        compiler_params=pltpu.CompilerParams(
            collective_id=0, has_side_effects=True, vmem_limit_bytes=56 * 1024 * 1024
        ),
    )(
        history[0], z_weight, xbc_weight, dt_weight.T, dt_bias, a_log, conv_weight,
        conv_bias, d_skip, norm_gain, out_weight, label_pos, label_count,
        label_value, item_feat[0], first_weight, second_weight,
    )
    chunks = 8
    enc, logit, second, wide = pl.pallas_call(
        functools.partial(widen, chunks),
        out_shape=(
            jax.ShapeDtypeStruct((rows, width), BF16),
            jax.ShapeDtypeStruct((1, slots), F32),
            jax.ShapeDtypeStruct((hid // 128, 128), F32),
            jax.ShapeDtypeStruct((fan, hid), F32),
        ),
        in_specs=[hbm] * 4,
        out_specs=(hbm,) * 4,
        scratch_shapes=[
            vm((chunks, blocks // chunks, RB, TILE)), vm((chunks, fan // chunks, hid), F32),
            pltpu.SemaphoreType.DMA((chunks,)), pltpu.SemaphoreType.DMA((chunks + 3,)),
        ],
        compiler_params=pltpu.CompilerParams(vmem_limit_bytes=56 * 1024 * 1024),
    )(enc, logit, second, grads)
    return enc[None], logit, wide, second.reshape(hid)


def solution(mesh):
    row = P(("grp", "user"), "tm", None)
    row2 = P(("grp", "user"), "tm")
    in_specs = (row,) + (P(),) * 10 + (row2, row2, row2, row, P(), P())
    out_specs = (row, row2, P("grp", None), P("grp"))
    return jax.shard_map(
        functools.partial(body, mesh.shape["tm"], mesh.shape["user"]),
        mesh=mesh, in_specs=in_specs, out_specs=out_specs, check_vma=False,
    )
```
